32 devices in a mesh: grp: 2 (over y), ta: 16 (over z, x, core).
Axes of the slice: x: 2, y: 2, z: 4, core: 2. Of those that a mesh axis runs over, the one named last changes fastest.
Arguments:
- perambulator: bfloat16 [2, 16, 768, 2, 512], P('grp', None, 'ta'), parts along dimension 0, may hold values from -1.1953125 to 1.1953125
- batch_columns: int32 [32], P(('grp', 'ta')), parts along dimension 0, may hold values from 1 to 48, 512 in all
- sink_operator: int32 [2, 16], replicated, may hold values from 0 to 1
- sink_elemental: bfloat16 [8, 16, 2, 128, 128], P('grp'), parts along dimension 0, may hold values from -0.375 to 0.375
- source_elemental: bfloat16 [2, 2, 128, 128], P('grp'), parts along dimension 0, may hold values from -0.375 to 0.375
Outputs:
- loops: bfloat16 [32, 2, 512, 512], P(('grp', 'ta')), parts along dimension 0
The draws below stay inside these ranges and needn't reach their ends.
There are 2 independent parts, one for each index of `grp`. The reference program is written for one: setup_inputs(seed, part) draws one part's arguments, and reference() takes and returns one part's arrays. A program takes and returns all parts, laid end to end along the dimension named above; an argument that names none is the same for every part. Nothing has to cross between parts.
Inputs may be any that keep to these rules, and one draw needn't show every extreme that they name: Batch d holds columns starts[d] to starts[d] + batch_columns[d] - 1 of every source and sink time, in order, in its first batch_columns[d] slots; later slots hold nothing that is read. The entries sum to 512 and the largest equals 48.
All inputs are finite; a program needn't handle non-finite values. No bound on the sum of `batch_columns` on one device may be relied on, other than what follows from the above.
Results may differ from the reference program's by a relative error of at most 0.0057.
Values may be sent and summed in bfloat16 or wider, within the bound.
A program may use at most 64 MiB of HBM per device.

```python
import math
import jax
import jax.numpy as jnp
import numpy as np
from jax import lax

NEV = 128
NSNK = 16
NDISP = 2
ORDER = 512
NSRC = 1
CAPN = 48
SLOTS = 768
NOPS = 4
N_TA = 16


def plant(values, key, low, high):
    longest = values.shape.index(max(values.shape))
    spots = []
    for shift in (0, 1):
        where = [jax.random.randint(jax.random.fold_in(key, axis), (), 0, length) for axis, length in enumerate(values.shape)]
        where[longest] = (where[longest] + shift) % values.shape[longest]
        spots.append(tuple(where))
    return values.at[spots[0]].set(low).at[spots[1]].set(high)


def shard_levels(stream_key, dims, cuts, least, high):
    factor_of, own = 1.0, jax.random.fold_in(stream_key, 6)
    for axis_at, blocks in cuts:
        draws = jnp.exp(jax.random.uniform(jax.random.fold_in(own, axis_at), (blocks,), jnp.float32, least / len(cuts), high / len(cuts)))
        factor_of = factor_of * jnp.repeat(draws, dims[axis_at] // blocks).reshape([-1 if axis == axis_at else 1 for axis in range(len(dims))])
    return factor_of


def profile(amount, total, limit, slope):
    loads = [(1 << 20) // math.isqrt(rank ** slope) + 1 for rank in range(2, amount + 1)]
    surplus, holding = total - limit - (amount - 1), [1] * (amount - 1)
    while surplus > 0:
        candidates = [i for i in range(amount - 1) if holding[i] < limit]
        pool, budget = sum([loads[i] for i in candidates]), surplus
        for i in candidates:
            addition = min(limit - holding[i], max(1, budget * loads[i] // pool), surplus)
            holding[i] = holding[i] + addition
            surplus = surplus - addition
    return np.array([limit] + holding)


def ragged_sizes(stream_key, count, total, limit, slope):
    if count == 2:
        one = jax.random.randint(stream_key, (), max(1, total - limit), min(limit, total - 1) + 1)
        return jnp.stack([one, total - one])
    sizes = jnp.asarray(profile(count, total, limit, slope), jnp.int32)
    twos = (count - 1) // 2
    source_of, sink = sizes[1:1 + 2 * twos:2], sizes[2:2 + 2 * twos:2]
    margin = jnp.minimum(source_of - 1, limit - sink)
    moved = jax.random.randint(jax.random.fold_in(stream_key, 1), (twos,), 0, 1 << 20) % (margin + 1)
    sizes = sizes.at[1:1 + 2 * twos:2].set(source_of - moved).at[2:2 + 2 * twos:2].set(sink + moved)
    return sizes[jax.random.permutation(jax.random.fold_in(stream_key, 2), count)]


def gaussian(rng, extent, deviation, reach, pieces=(), kind=jnp.bfloat16):
    level = shard_levels(rng, extent, pieces, -0.22, 0.18) if pieces else 1.0
    result = jax.random.normal(rng, extent, jnp.float32) * deviation * level
    return jnp.minimum(jnp.maximum(result, -reach), reach).astype(kind)


def setup_inputs(seed: int = 0, part: int = 0) -> dict:
    key_list = jax.random.split(jax.random.key(seed), 6)
    own_keys = jax.random.split(jax.random.fold_in(key_list[5], part), 6)
    perambulator = gaussian(own_keys[0], (NSRC, NSNK, SLOTS, 2, ORDER), 0.2, 1.1953125, ((2, 16),))
    batch_columns = ragged_sizes(own_keys[1], N_TA, ORDER, CAPN, 2).astype(jnp.int32)
    sink_operator = plant(jax.random.randint(key_list[2], (2, NSNK), 0, 2), jax.random.fold_in(key_list[2], 1), 0, 1).astype(jnp.int32)
    sink_elemental = gaussian(own_keys[3], (NOPS, NSNK, 2, NEV, NEV), (2 * NEV) ** -0.5, 0.375)
    source_elemental = gaussian(own_keys[4], (NSRC, 2, NEV, NEV), (2 * NEV) ** -0.5, 0.375)
    return dict(perambulator=perambulator, batch_columns=batch_columns, sink_operator=sink_operator, sink_elemental=sink_elemental, source_elemental=source_elemental)


def spin_signs():
    spin = jnp.arange(4 * NEV, dtype=jnp.int32) // NEV
    return jnp.where(spin < 2, 1.0, -1.0).astype(jnp.float32)


def column_slots(batch_columns):
    starts = jnp.cumsum(batch_columns) - batch_columns
    column = jnp.arange(ORDER, dtype=jnp.int32)
    holder = jnp.sum((starts[None, :] <= column[:, None]).astype(jnp.int32), axis=1) - 1
    first = jnp.take(starts, holder)
    return (holder * CAPN + column - first).astype(jnp.int32)


def product_t(left, right):
    return jnp.dot(left, right.T, preferred_element_type=jnp.float32)


def pair_loop(columns, e_real, e_imag, f_real, f_imag, signs):
    p_real = columns[:, 0, :]
    p_imag = columns[:, 1, :]
    flat_real = p_real.reshape(ORDER * 4, NEV)
    flat_imag = p_imag.reshape(ORDER * 4, NEV)
    x_real = (product_t(flat_real, e_real) - product_t(flat_imag, e_imag)).reshape(ORDER, ORDER)
    x_imag = (product_t(flat_real, e_imag) + product_t(flat_imag, e_real)).reshape(ORDER, ORDER)
    x_real = (x_real * signs[None, :]).astype(jnp.bfloat16)
    x_imag = (x_imag * signs[None, :]).astype(jnp.bfloat16)
    cube_real = p_real.reshape(4, NEV, ORDER).astype(jnp.float32)
    cube_imag = p_imag.reshape(4, NEV, ORDER).astype(jnp.float32)
    fr = f_real.astype(jnp.float32)
    fi = f_imag.astype(jnp.float32)
    y_real = jnp.einsum("ij,sjk->sik", fr, cube_real) + jnp.einsum("ij,sjk->sik", fi, cube_imag)
    y_imag = jnp.einsum("ij,sjk->sik", fi, cube_real) - jnp.einsum("ij,sjk->sik", fr, cube_imag)
    y_real = (y_real * signs[None, None, :]).reshape(ORDER, ORDER).astype(jnp.bfloat16)
    y_imag = (y_imag * signs[None, None, :]).reshape(ORDER, ORDER).astype(jnp.bfloat16)
    left_real = x_real.T
    left_imag = x_imag.T
    m_real = jnp.dot(left_real, y_real, preferred_element_type=jnp.float32) - jnp.dot(left_imag, y_imag, preferred_element_type=jnp.float32)
    m_imag = jnp.dot(left_real, y_imag, preferred_element_type=jnp.float32) + jnp.dot(left_imag, y_real, preferred_element_type=jnp.float32)
    return jnp.stack([m_real, m_imag], 0).astype(jnp.bfloat16)


def reference(perambulator, batch_columns, sink_operator, sink_elemental, source_elemental):
    slot_index = column_slots(batch_columns)
    signs = spin_signs()

    def one_pair(pair_index):
        source = pair_index // NSNK
        sink_time = pair_index % NSNK
        block_pair = perambulator[source, sink_time]
        columns = jnp.take(block_pair, slot_index, axis=0)
        operator = sink_operator[0, sink_time] * NDISP + sink_operator[1, sink_time]
        element = sink_elemental[operator, sink_time]
        source_table = source_elemental[source]
        return pair_loop(columns, element[0], element[1], source_table[0], source_table[1], signs)

    return lax.map(one_pair, jnp.arange(NSRC * NSNK, dtype=jnp.int32))
```

```python
import functools

import jax
import jax.numpy as jnp
from jax import lax
from jax.experimental import pallas as pl
from jax.experimental.pallas import tpu as pltpu
from jax.sharding import PartitionSpec as P

NDISP = 2
MESH = pl.DeviceIdType.MESH


def product(left, right, contracted=((1,), (0,))):
    return lax.dot_general(left, right, (contracted, ((), ())), preferred_element_type=jnp.float32)


def kernel(
    devices, sink_count, capacity, group,
    blocks_ref, count_ref, operator_ref, sink_ref, source_ref, out_ref,
    recv, counts, starts, acc, prop_re, prop_im, x_re, x_im, y_re, y_im, y_neg, elems, table,
    send_sem, recv_sem, count_send, count_recv, local_sem,
):
    me = lax.axis_index("ta")
    rows, order = recv.shape[1], recv.shape[2]
    eigen = order // 4
    sink_time = lax.rem(me, sink_count)
    source = me // sink_count

    own = pltpu.make_async_copy(blocks_ref.at[me], recv.at[me], local_sem.at[0])
    own.start()
    fetch_sink = pltpu.make_async_copy(sink_ref.at[:, sink_time], elems, local_sem.at[1])
    fetch_sink.start()
    fetch_source = pltpu.make_async_copy(source_ref.at[source], table, local_sem.at[2])
    fetch_source.start()

    counts[me] = jnp.full(counts.shape[1:], count_ref[0], jnp.int32)

    def peer(step):
        half = (step + 1) // 2
        return devices // 2 + half * (1 - 2 * lax.rem(step, 2))

    barrier = pltpu.get_barrier_semaphore()

    @pl.loop(1, devices)
    def _(k):
        pl.semaphore_signal(barrier, inc=1, device_id={"ta": lax.rem(me + k, devices)}, device_id_type=MESH)

    pl.semaphore_wait(barrier, devices - 1)

    def block_copy(target, slot):
        return pltpu.make_async_remote_copy(
            src_ref=blocks_ref.at[target], dst_ref=recv.at[slot],
            send_sem=send_sem.at[target], recv_sem=recv_sem.at[slot],
            device_id={"ta": target}, device_id_type=MESH,
        )

    def count_copy(target, slot):
        return pltpu.make_async_remote_copy(
            src_ref=counts.at[me], dst_ref=counts.at[slot],
            send_sem=count_send.at[target], recv_sem=count_recv.at[slot],
            device_id={"ta": target}, device_id_type=MESH,
        )

    @pl.loop(1, devices)
    def _(k):
        count_copy(lax.rem(me + k, devices), me).start()

    @pl.loop(0, devices - 1)
    def _(step):
        block_copy(lax.rem(me + peer(step), devices), me).start()

    acc[...] = jnp.zeros_like(acc)
    fetch_source.wait()
    fetch_sink.wait()
    own.wait()

    @pl.loop(1, devices)
    def _(k):
        count_copy(me, lax.rem(me + k, devices)).wait_recv()

    def running(d, total):
        starts[d] = total
        return total + counts[d]

    lax.fori_loop(0, devices, running, jnp.zeros(counts.shape[1:], jnp.int32))

    operator = operator_ref[0, sink_time] * NDISP + operator_ref[1, sink_time]
    element = elems[operator]
    e_real, e_imag = element[0], element[1]
    e_full = jnp.concatenate(
        [jnp.concatenate([e_real, -e_imag], 1), jnp.concatenate([e_imag, e_real], 1)], 0
    )
    f_real, f_imag = table[0], table[1]
    f_full = jnp.concatenate(
        [jnp.concatenate([f_real, f_imag], 1), jnp.concatenate([f_imag, -f_real], 1)], 0
    )

    group_count = devices // group
    my_group = me // group
    width = group * rows
    lane = lax.broadcasted_iota(jnp.int32, (8, width), 1)
    lane_batch = lane // rows
    lane_row = lane - lane_batch * rows
    lane_slot = lane_row // 2
    lane_part = lane_row - lane_slot * 2
    tile = 2 * eigen

    @pl.loop(0, group_count)
    def _(step):
        which = lax.rem(my_group + step, group_count)
        first = which * group

        for g in range(group):
            @pl.when(first + g != me)
            def _():
                block_copy(me, first + g).wait_recv()

        held = jnp.zeros((8, width), jnp.int32)
        begin = jnp.zeros((8, width), jnp.int32)
        for g in range(group):
            here = lane_batch == g
            held = jnp.where(here, counts[first + g][0:1, 0:1], held)
            begin = jnp.where(here, starts[first + g][0:1, 0:1], begin)
        goal = jnp.where(lane_slot < held, lane_part * order + begin + lane_slot, -1)[0:1]
        arrived = recv[pl.ds(first, group)].reshape(width, order)
        for m in range(0, 2 * order, tile):
            index = lax.broadcasted_iota(jnp.int32, (tile, width), 0) + m
            picks = jnp.where(index == goal, 1.0, 0.0).astype(jnp.bfloat16)
            acc[m:m + tile] += product(picks, arrived)

    prop_re[...] = acc[0:order].astype(jnp.bfloat16)
    prop_im[...] = acc[order:2 * order].astype(jnp.bfloat16)

    for s in range(4):
        span = slice(s * eigen, (s + 1) * eigen)
        sign = 1.0 if s < 2 else -1.0
        pair = jnp.concatenate([prop_re[:, span], prop_im[:, span]], 1)
        x = product(e_full, pair, ((1,), (1,))) * sign
        x_re[span] = x[:eigen].astype(jnp.bfloat16)
        x_im[span] = x[eigen:].astype(jnp.bfloat16)

    spin = lax.broadcasted_iota(jnp.int32, (1, order), 1) // eigen
    signs = jnp.where(spin < 2, 1.0, -1.0).astype(jnp.float32)
    for t in range(4):
        span = slice(t * eigen, (t + 1) * eigen)
        stacked = jnp.concatenate([prop_re[span], prop_im[span]], 0)
        y = product(f_full, stacked) * signs
        y_re[span] = y[:eigen].astype(jnp.bfloat16)
        y_im[span] = y[eigen:].astype(jnp.bfloat16)
        y_neg[span] = (-y[eigen:]).astype(jnp.bfloat16)

    for m in range(0, order, tile):
        left_re, left_im = x_re[m:m + tile], x_im[m:m + tile]
        out_ref[0, 0, m:m + tile] = (product(left_re, y_re[...]) + product(left_im, y_neg[...])).astype(jnp.bfloat16)
        out_ref[0, 1, m:m + tile] = (product(left_re, y_im[...]) + product(left_im, y_re[...])).astype(jnp.bfloat16)

    @pl.loop(1, devices)
    def _(k):
        target = lax.rem(me + k, devices)
        count_copy(target, me).wait_send()
        block_copy(target, me).wait_send()


def local(perambulator, batch_columns, sink_operator, sink_elemental, source_elemental):
    source_count, sink_count, capacity, _, order = perambulator.shape
    devices = lax.axis_size("ta")
    pairs = source_count * sink_count
    eigen = order // 4
    blocks = perambulator.reshape(pairs, capacity * 2, order)
    extra = -(capacity * 2) % 16
    if extra:
        blocks = jnp.pad(blocks, ((0, 0), (0, extra), (0, 0)))
    rows = capacity * 2 + extra
    group = max(g for g in range(1, devices + 1) if devices % g == 0 and (g == 1 or g * rows <= 256))
    operators = sink_elemental.shape[0]
    vmem = pl.BlockSpec(memory_space=pltpu.VMEM)
    smem = pl.BlockSpec(memory_space=pltpu.SMEM)
    hbm = pl.BlockSpec(memory_space=pl.ANY)
    square = pltpu.VMEM((order, order), jnp.bfloat16)
    return pl.pallas_call(
        functools.partial(kernel, devices, sink_count, capacity, group),
        out_shape=jax.ShapeDtypeStruct((1, 2, order, order), jnp.bfloat16),
        in_specs=[hbm, smem, smem, hbm, hbm],
        out_specs=vmem,
        scratch_shapes=[
            pltpu.VMEM((devices, rows, order), jnp.bfloat16),
            pltpu.VMEM((devices, 8, 128), jnp.int32),
            pltpu.VMEM((devices, 8, 128), jnp.int32),
            pltpu.VMEM((2 * order, order), jnp.float32),
            square, square, square, square, square, square, square,
            pltpu.VMEM((operators, 2, eigen, eigen), jnp.bfloat16),
            pltpu.VMEM((2, eigen, eigen), jnp.bfloat16),
            pltpu.SemaphoreType.DMA((devices,)),
            pltpu.SemaphoreType.DMA((devices,)),
            pltpu.SemaphoreType.DMA((devices,)),
            pltpu.SemaphoreType.DMA((devices,)),
            pltpu.SemaphoreType.DMA((3,)),
        ],
        compiler_params=pltpu.CompilerParams(
            collective_id=0, has_side_effects=True, vmem_limit_bytes=40 * 1024 * 1024
        ),
    )(blocks, batch_columns, sink_operator, sink_elemental, source_elemental)


def solution(mesh):
    placed = (
        P("grp", None, "ta", None, None),
        P(("grp", "ta")),
        P(),
        P("grp", None, None, None, None),
        P("grp", None, None, None),
    )
    return jax.shard_map(
        local,
        mesh=mesh,
        in_specs=placed,
        out_specs=P(("grp", "ta"), None, None, None),
        check_vma=False,
    )
```

```python
import functools

import jax
import jax.numpy as jnp
from jax import lax
from jax.experimental import pallas as pl
from jax.experimental.pallas import tpu as pltpu
from jax.sharding import PartitionSpec as P

NDISP = 2
MESH = pl.DeviceIdType.MESH


def product(left, right, contracted=((1,), (0,))):
    return lax.dot_general(left, right, (contracted, ((), ())), preferred_element_type=jnp.float32)


def kernel(
    devices, sink_count, capacity, group,
    blocks_ref, count_ref, operator_ref, sink_ref, source_ref, out_ref,
    recv, counts, starts, acc, prop_re, prop_im, x_re, x_im, y_re, y_im, y_neg, elems, table,
    send_sem, recv_sem, count_send, count_recv, local_sem,
):
    me = lax.axis_index("ta")
    rows, order = 2 * recv.shape[1], recv.shape[3]
    eigen = order // 4
    sink_time = lax.rem(me, sink_count)
    source = me // sink_count

    own = pltpu.make_async_copy(blocks_ref.at[me], recv.at[me], local_sem.at[0])
    own.start()
    fetch_sink = pltpu.make_async_copy(sink_ref.at[:, sink_time], elems, local_sem.at[1])
    fetch_sink.start()
    fetch_source = pltpu.make_async_copy(source_ref.at[source], table, local_sem.at[2])
    fetch_source.start()

    counts[me] = jnp.full(counts.shape[1:], count_ref[0], jnp.int32)

    def peer(step):
        return step + 1

    barrier = pltpu.get_barrier_semaphore()

    @pl.loop(1, devices)
    def _(k):
        pl.semaphore_signal(barrier, inc=1, device_id={"ta": lax.rem(me + k, devices)}, device_id_type=MESH)

    pl.semaphore_wait(barrier, devices - 1)

    def block_copy(target, slot):
        return pltpu.make_async_remote_copy(
            src_ref=blocks_ref.at[target], dst_ref=recv.at[slot],
            send_sem=send_sem.at[target], recv_sem=recv_sem.at[slot],
            device_id={"ta": target}, device_id_type=MESH,
        )

    def count_copy(target, slot):
        return pltpu.make_async_remote_copy(
            src_ref=counts.at[me], dst_ref=counts.at[slot],
            send_sem=count_send.at[target], recv_sem=count_recv.at[slot],
            device_id={"ta": target}, device_id_type=MESH,
        )

    @pl.loop(1, devices)
    def _(k):
        count_copy(lax.rem(me + k, devices), me).start()

    @pl.loop(0, devices - 1)
    def _(step):
        block_copy(lax.rem(me + peer(step), devices), me).start()

    acc[...] = jnp.zeros_like(acc)
    fetch_source.wait()
    fetch_sink.wait()
    own.wait()

    @pl.loop(1, devices)
    def _(k):
        count_copy(me, lax.rem(me + k, devices)).wait_recv()

    def running(d, total):
        starts[d] = total
        return total + counts[d]

    lax.fori_loop(0, devices, running, jnp.zeros(counts.shape[1:], jnp.int32))

    operator = operator_ref[0, sink_time] * NDISP + operator_ref[1, sink_time]
    element = elems[operator]
    e_real, e_imag = element[0], element[1]
    e_full = jnp.concatenate(
        [jnp.concatenate([e_real, -e_imag], 1), jnp.concatenate([e_imag, e_real], 1)], 0
    )
    f_real, f_imag = table[0], table[1]
    f_full = jnp.concatenate(
        [jnp.concatenate([f_real, f_imag], 1), jnp.concatenate([f_imag, -f_real], 1)], 0
    )

    group_count = devices // group
    my_group = me // group
    width = group * rows
    lane = lax.broadcasted_iota(jnp.int32, (8, width), 1)
    lane_batch = lane // rows
    lane_row = lane - lane_batch * rows
    lane_slot = lane_row // 2
    lane_part = lane_row - lane_slot * 2
    tile = 2 * eigen

    @pl.loop(0, group_count)
    def _(step):
        which = lax.rem(my_group + step, group_count)
        first = which * group

        for g in range(group):
            @pl.when(first + g != me)
            def _():
                block_copy(me, first + g).wait_recv()

        held = jnp.zeros((8, width), jnp.int32)
        begin = jnp.zeros((8, width), jnp.int32)
        for g in range(group):
            here = lane_batch == g
            held = jnp.where(here, counts[first + g][0:1, 0:1], held)
            begin = jnp.where(here, starts[first + g][0:1, 0:1], begin)
        goal = jnp.where(lane_slot < held, lane_part * order + begin + lane_slot, -1)[0:1]
        arrived = recv[pl.ds(first, group)].reshape(width, order)
        for m in range(0, 2 * order, tile):
            index = lax.broadcasted_iota(jnp.int32, (tile, width), 0) + m
            picks = jnp.where(index == goal, 1.0, 0.0).astype(jnp.bfloat16)
            acc[m:m + tile] += product(picks, arrived)

    prop_re[...] = acc[0:order].astype(jnp.bfloat16)
    prop_im[...] = acc[order:2 * order].astype(jnp.bfloat16)

    for s in range(4):
        span = slice(s * eigen, (s + 1) * eigen)
        sign = 1.0 if s < 2 else -1.0
        pair = jnp.concatenate([prop_re[:, span], prop_im[:, span]], 1)
        x = product(e_full, pair, ((1,), (1,))) * sign
        x_re[span] = x[:eigen].astype(jnp.bfloat16)
        x_im[span] = x[eigen:].astype(jnp.bfloat16)

    spin = lax.broadcasted_iota(jnp.int32, (1, order), 1) // eigen
    signs = jnp.where(spin < 2, 1.0, -1.0).astype(jnp.float32)
    for t in range(4):
        span = slice(t * eigen, (t + 1) * eigen)
        stacked = jnp.concatenate([prop_re[span], prop_im[span]], 0)
        y = product(f_full, stacked) * signs
        y_re[span] = y[:eigen].astype(jnp.bfloat16)
        y_im[span] = y[eigen:].astype(jnp.bfloat16)
        y_neg[span] = (-y[eigen:]).astype(jnp.bfloat16)

    for m in range(0, order, tile):
        left_re, left_im = x_re[m:m + tile], x_im[m:m + tile]
        out_ref[0, 0, m:m + tile] = (product(left_re, y_re[...]) + product(left_im, y_neg[...])).astype(jnp.bfloat16)
        out_ref[0, 1, m:m + tile] = (product(left_re, y_im[...]) + product(left_im, y_re[...])).astype(jnp.bfloat16)

    @pl.loop(1, devices)
    def _(k):
        target = lax.rem(me + k, devices)
        count_copy(target, me).wait_send()
        block_copy(target, me).wait_send()


def local(perambulator, batch_columns, sink_operator, sink_elemental, source_elemental):
    source_count, sink_count, capacity, _, order = perambulator.shape
    devices = lax.axis_size("ta")
    pairs = source_count * sink_count
    eigen = order // 4
    blocks = perambulator.reshape(pairs, capacity, 2, order)
    extra = -(capacity * 2) % 16
    if extra:
        blocks = jnp.pad(blocks, ((0, 0), (0, extra // 2), (0, 0), (0, 0)))
    rows = capacity * 2 + extra
    group = max(g for g in range(1, devices + 1) if devices % g == 0 and (g == 1 or g * rows <= 256))
    operators = sink_elemental.shape[0]
    vmem = pl.BlockSpec(memory_space=pltpu.VMEM)
    smem = pl.BlockSpec(memory_space=pltpu.SMEM)
    hbm = pl.BlockSpec(memory_space=pl.ANY)
    square = pltpu.VMEM((order, order), jnp.bfloat16)
    return pl.pallas_call(
        functools.partial(kernel, devices, sink_count, capacity, group),
        out_shape=jax.ShapeDtypeStruct((1, 2, order, order), jnp.bfloat16),
        in_specs=[hbm, smem, smem, hbm, hbm],
        out_specs=vmem,
        scratch_shapes=[
            pltpu.VMEM((devices, rows // 2, 2, order), jnp.bfloat16),
            pltpu.VMEM((devices, 8, 128), jnp.int32),
            pltpu.VMEM((devices, 8, 128), jnp.int32),
            pltpu.VMEM((2 * order, order), jnp.float32),
            square, square, square, square, square, square, square,
            pltpu.VMEM((operators, 2, eigen, eigen), jnp.bfloat16),
            pltpu.VMEM((2, eigen, eigen), jnp.bfloat16),
            pltpu.SemaphoreType.DMA((devices,)),
            pltpu.SemaphoreType.DMA((devices,)),
            pltpu.SemaphoreType.DMA((devices,)),
            pltpu.SemaphoreType.DMA((devices,)),
            pltpu.SemaphoreType.DMA((3,)),
        ],
        compiler_params=pltpu.CompilerParams(
            collective_id=0, has_side_effects=True, vmem_limit_bytes=60 * 1024 * 1024
        ),
    )(blocks, batch_columns, sink_operator, sink_elemental, source_elemental)


def solution(mesh):
    placed = (
        P("grp", None, "ta", None, None),
        P(("grp", "ta")),
        P(),
        P("grp", None, None, None, None),
        P("grp", None, None, None),
    )
    return jax.shard_map(
        local,
        mesh=mesh,
        in_specs=placed,
        out_specs=P(("grp", "ta"), None, None, None),
        check_vma=False,
    )
```
